32 devices in a mesh: prow: 4 (over x, core), pcol: 8 (over z, y).
Axes of the slice: x: 2, y: 2, z: 4, core: 2. Of those that a mesh axis runs over, the one named last changes fastest.
Arguments:
- blocks: bfloat16 [20480, 128, 128], P(('prow', 'pcol')), may hold values from -0.078125 to 0.078125
- row_index: int32 [20480], P(('prow', 'pcol')), may hold values from 0 to 511, as said below
- col_index: int32 [20480], P(('prow', 'pcol')), may hold values from 0 to 511, as said below
- send_tiles: int32 [512], P(('prow', 'pcol')), may hold values from 0 to 511, as said below
- lighting: bfloat16 [65536, 384], P(('prow', 'pcol')), may hold values from -6 to 6
- albedo: float32 [3, 65536], P(None, ('pcol', 'prow')), may hold values from 0.2 to 0.95
- emission: bfloat16 [65536, 384], P(('pcol', 'prow')), may hold values from -4 to 4
Outputs:
- radiance: bfloat16 [65536, 384], P(('pcol', 'prow'))
The draws below stay inside these ranges and needn't reach their ends.
Inputs may be any that keep to these rules, and one draw needn't show every extreme that they name: `send_tiles`: group g (the blocks of device g) lists 16 distinct tiles in increasing order: exactly 4 from each of the 4 ranges of 16 block rows starting at c * 64 + r * 16, r = 0 .. 3, where c = g % 8. `row_index`: each block's row is one of its group's listed tiles, each listed tile has at least one block, and a group's blocks are ordered by row; counts per tile are uneven. `col_index`: the blocks of group g have columns in (g // 8) * 128 to (g // 8 + 1) * 128 - 1; a pair of row and column may repeat, and then the blocks add.
All inputs are finite; a program needn't handle non-finite values.
Results may differ from the reference program's by a relative error of at most 0.008.
Values may be sent and summed in bfloat16 or wider, within the bound.
A program may use at most 192 MiB of HBM per device.

```python
import jax
import jax.numpy as jnp
from jax import lax

TILE = 128
COLORS = 3
BASIS = 128
OWN_TILES = 16
BLK_DEV = 640
SEND_OWN = 4
COLS = 384
NSEND = 16
NB = 512
NPATCH = 65536
BLOCKS = 20480
N_PROW = 4
N_PCOL = 8
DEVICES = 32


def pattern(key):
    device_ids = jnp.arange(DEVICES)
    prow_ids = device_ids // N_PCOL
    pcol_ids = device_ids % N_PCOL
    scores = jax.random.randint(jax.random.fold_in(key, 11), (DEVICES, N_PROW, OWN_TILES), 0, 1 << 20) * OWN_TILES + jnp.arange(OWN_TILES)
    chosen = jnp.sort(jnp.argsort(scores, axis=-1)[..., :SEND_OWN], axis=-1)
    local = jnp.arange(N_PROW)[None, :, None] * OWN_TILES + chosen
    listed = (pcol_ids[:, None, None] * (OWN_TILES * N_PROW) + local).reshape(DEVICES, NSEND)
    first = jax.random.randint(jax.random.fold_in(key, 12), (DEVICES, BLK_DEV), 0, NSEND)
    second = jax.random.randint(jax.random.fold_in(key, 13), (DEVICES, BLK_DEV), 0, NSEND)
    slots = first * second // NSEND
    positions = jnp.arange(BLK_DEV)[None, :]
    slots = jnp.where(positions < NSEND, positions, slots)
    slots = jnp.sort(slots, axis=-1)
    rows = jnp.take_along_axis(listed, slots, axis=1)
    offsets = jax.random.randint(jax.random.fold_in(key, 14), (DEVICES, BLK_DEV), 0, OWN_TILES * N_PCOL)
    columns = prow_ids[:, None] * (OWN_TILES * N_PCOL) + offsets
    return (listed.reshape(-1).astype(jnp.int32), rows.reshape(-1).astype(jnp.int32), columns.reshape(-1).astype(jnp.int32))


def draw_send_tiles(key, part):
    return pattern(key)[0]


def draw_row_index(key, part):
    return pattern(key)[1]


def draw_col_index(key, part):
    return pattern(key)[2]


def steps_of(own_key, shape, pieces, low, high):
    loudness = 1.0
    for axis_at, blocks in pieces:
        draws = jax.random.uniform(jax.random.fold_in(jax.random.fold_in(own_key, 6), axis_at), (blocks,), jnp.float32, low / len(pieces), high / len(pieces))
        loudness = loudness * jnp.repeat(jnp.exp(draws), shape[axis_at] // blocks).reshape((-1,) + (1,) * (len(shape) - 1 - axis_at))
    return loudness


def gaussian(stream_key, shape, scale, bound, cuts=(), dtype=jnp.bfloat16):
    drawn = jax.random.normal(stream_key, shape, jnp.float32) * scale
    if len(cuts) > 0:
        drawn = steps_of(stream_key, shape, cuts, -0.22, 0.18) * drawn
    return jnp.clip(drawn, min=-bound, max=bound).astype(dtype)


def setup_inputs(seed: int = 0) -> dict:
    splits = jax.random.split(jax.random.key(seed), 8)
    blocks = gaussian(splits[0], (BLOCKS, TILE, TILE), (TILE * BLK_DEV // OWN_TILES) ** -0.5, 0.078125, ((0, 32),))
    row_index = draw_row_index(jax.random.fold_in(splits[7], 71), 0)
    col_index = draw_col_index(jax.random.fold_in(splits[7], 71), 0)
    send_tiles = draw_send_tiles(jax.random.fold_in(splits[7], 71), 0)
    lighting = gaussian(splits[4], (NPATCH, COLS), 1.0, 6.0, ((0, 32),))
    albedo = jnp.clip(0.2 + 0.75 * jax.random.uniform(splits[5], (COLORS, NPATCH), jnp.float32) ** steps_of(splits[5], (COLORS, NPATCH), ((1, 32),), -0.2, 0.2), 0.2, 0.95)
    emission = gaussian(splits[6], (NPATCH, COLS), 0.5, 4.0, ((0, 32),))
    return dict(blocks=blocks, row_index=row_index, col_index=col_index, send_tiles=send_tiles, lighting=lighting, albedo=albedo, emission=emission)


def reference(blocks, row_index, col_index, send_tiles, lighting, albedo, emission):
    tiles = lighting.reshape(NB, TILE, COLS)
    grouped = blocks.reshape(DEVICES, BLK_DEV, TILE, TILE)
    rows = row_index.reshape(DEVICES, BLK_DEV).astype(jnp.int32)
    columns = col_index.reshape(DEVICES, BLK_DEV).astype(jnp.int32)
    listed = send_tiles.reshape(DEVICES, NSEND).astype(jnp.int32)

    def one_group(running, items):
        block_set, row_set, col_set, list_set = items
        slots = jnp.sum((list_set[None, :] < row_set[:, None]).astype(jnp.int32), axis=1)
        product = jnp.einsum("gpq,gqk->gpk", block_set.astype(jnp.float32), tiles[col_set].astype(jnp.float32))
        part = jax.ops.segment_sum(product, slots, num_segments=NSEND).astype(jnp.bfloat16)
        part = lax.optimization_barrier(part).astype(jnp.float32)
        return running.at[list_set].add(part), None

    start = jnp.zeros((NB, TILE, COLS), jnp.float32)
    gathered, _ = lax.scan(one_group, start, (grouped, rows, columns, listed))
    lit = gathered.reshape(NPATCH, COLORS, BASIS) * jnp.transpose(albedo)[:, :, None]
    return (lit.reshape(NPATCH, COLS) + emission.astype(jnp.float32)).astype(jnp.bfloat16)
```

```python
import functools

import jax
import jax.numpy as jnp
from jax import lax
from jax.experimental import pallas as pl
from jax.experimental.pallas import tpu as pltpu
from jax.sharding import PartitionSpec as P

GROUP = 8
MESH = pl.DeviceIdType.MESH


def ring_place(pcol, n):
    odd = pcol % 2
    return (1 - odd) * (pcol // 2) + odd * (n - 1 - pcol // 2)


def ring_device(place, n):
    late = place // (n // 2)
    return (1 - late) * (2 * place) + late * (2 * (n - 1 - place) + 1)


def fused(
    n,
    rows,
    colours,
    plan_ref,
    last_ref,
    col_ref,
    ids_ref,
    blocks_ref,
    light_ref,
    arr_ref,
    got_ref,
    *scratch,
):
    slabs = scratch[:colours]
    parts = scratch[colours : 2 * colours]
    blk, sums, ring_send, ring_recv, own_sem, blk_sem, ex_send, ex_recv, ex_own, id_send, id_recv, id_own = scratch[
        2 * colours :
    ]
    count = blocks_ref.shape[0]
    groups = plan_ref.shape[1]
    tiles = light_ref.shape[0]
    half = tiles // 2
    listed = last_ref.shape[0]
    per = listed // rows
    basis = slabs[0].shape[2]
    prow = lax.axis_index("prow")
    pcol = lax.axis_index("pcol")
    place = ring_place(pcol, n)
    after = ring_device((place + 1) % n, n)
    before = ring_device((place + n - 1) % n, n)
    messages = n - 1

    barrier = pltpu.get_barrier_semaphore()
    for side in (after, before):
        pl.semaphore_signal(barrier, inc=1, device_id={"pcol": side}, device_id_type=MESH)
    for d in range(1, rows):
        pl.semaphore_signal(barrier, inc=1, device_id={"prow": (prow + d) % rows}, device_id_type=MESH)

    own = [
        pltpu.make_async_copy(
            light_ref.at[:, :, pl.ds(c * basis, basis)], slabs[c].at[pl.ds(pcol * tiles, tiles)], own_sem.at[c]
        )
        for c in range(colours)
    ]
    for copy in own:
        copy.start()
    pl.semaphore_wait(barrier, 2 + rows - 1)

    def piece(c, m, way, arriving):
        step = m // 2
        part = (m + way) % 2
        if way == 0:
            source = (place + n - step - arriving) % n
        else:
            source = (place + step + arriving) % n
        at = ring_device(source, n) * tiles + part * half
        window = slabs[c].at[pl.ds(at, half)]
        return pltpu.make_async_remote_copy(
            src_ref=window,
            dst_ref=window,
            send_sem=ring_send.at[way, c, m],
            recv_sem=ring_recv.at[way, c, m],
            device_id={"pcol": before if way else after},
            device_id_type=MESH,
        )

    def to_row(c, d):
        target = (prow + d) % rows
        return pltpu.make_async_remote_copy(
            src_ref=parts[c].at[pl.ds(target * per, per)],
            dst_ref=arr_ref.at[c, prow],
            send_sem=ex_send.at[c, d],
            recv_sem=ex_recv.at[c, d],
            device_id={"prow": target},
            device_id_type=MESH,
        )

    def from_row(c, d):
        origin = (prow + rows - d) % rows
        return pltpu.make_async_remote_copy(
            src_ref=parts[c].at[pl.ds(0, per)],
            dst_ref=arr_ref.at[c, origin],
            send_sem=ex_send.at[c, d],
            recv_sem=ex_recv.at[c, d],
            device_id={"prow": origin},
            device_id_type=MESH,
        )

    def ids_to(d):
        target = (prow + d) % rows
        return pltpu.make_async_remote_copy(
            src_ref=ids_ref,
            dst_ref=got_ref.at[prow],
            send_sem=id_send.at[d],
            recv_sem=id_recv.at[d],
            device_id={"prow": target},
            device_id_type=MESH,
        )

    def ids_from(d):
        origin = (prow + rows - d) % rows
        return pltpu.make_async_remote_copy(
            src_ref=ids_ref,
            dst_ref=got_ref.at[origin],
            send_sem=id_send.at[d],
            recv_sem=id_recv.at[d],
            device_id={"prow": origin},
            device_id_type=MESH,
        )

    load = pltpu.make_async_copy(blocks_ref, blk.at[pl.ds(0, count)], blk_sem)

    def compute(c, low, high):
        def one(i, running):
            base = plan_ref[0, i]
            end = plan_ref[1, i]
            keep = plan_ref[2, i].astype(jnp.float32)
            left, right = [], []
            for j in range(GROUP):
                at = base + j
                inside = at < end
                left.append(blk[jnp.where(inside, at, count)])
                right.append(slabs[c][col_ref[jnp.where(inside, at, 0)]])
            running = running * keep + jnp.dot(
                jnp.concatenate(left, axis=1),
                jnp.concatenate(right, axis=0),
                preferred_element_type=jnp.float32,
            )
            sums[i + 1] = running
            return running

        lax.fori_loop(low, high, one, sums[low])

    def exchange(c):
        for s in range(listed):
            parts[c][s] = sums[last_ref[s]].astype(jnp.bfloat16)
        for d in range(1, rows):
            to_row(c, d).start()
        pltpu.make_async_copy(parts[c].at[pl.ds(prow * per, per)], arr_ref.at[c, prow], ex_own.at[c]).start()

    def finish_ring(c):
        for m in range(max(messages - 2, 0), messages):
            for way in (0, 1):
                piece(c, m, way, 1).wait_recv()

    cuts = [groups * k // (messages - 1) for k in range(messages)]
    for c in range(colours):
        own[c].wait()
        for m in range(messages):
            for way in (0, 1):
                if m >= 2:
                    piece(c, m - 2, way, 1).wait_recv()
                piece(c, m, way, 0).start()
            if c == 0 and m == 1:
                load.start()
                blk[count] = jnp.zeros(blk.shape[1:], blk.dtype)
                sums[0] = jnp.zeros(sums.shape[1:], sums.dtype)
                for d in range(1, rows):
                    ids_to(d).start()
                pltpu.make_async_copy(ids_ref, got_ref.at[prow], id_own).start()
            if c >= 1 and m >= 1:
                if m == 1:
                    if c == 1:
                        load.wait()
                    finish_ring(c - 1)
                compute(c - 1, cuts[m - 1], cuts[m])
                if m == messages - 1:
                    exchange(c - 1)
    finish_ring(colours - 1)
    compute(colours - 1, 0, groups)
    exchange(colours - 1)
    for c in range(colours):
        for m in range(messages):
            for way in (0, 1):
                piece(c, m, way, 0).wait_send()
        for d in range(1, rows):
            to_row(c, d).wait_send()
            from_row(c, d).wait_recv()
        pltpu.make_async_copy(parts[c].at[pl.ds(prow * per, per)], arr_ref.at[c, prow], ex_own.at[c]).wait()
    for d in range(1, rows):
        ids_to(d).wait_send()
        ids_from(d).wait_recv()
    pltpu.make_async_copy(ids_ref, got_ref.at[prow], id_own).wait()


def finish(share, here_ref, arr_ref, albedo_ref, emission_ref, out_ref, total):
    colours, rows, per = arr_ref.shape[:3]
    step = pl.program_id(0)
    total[...] = jnp.zeros_like(total)
    for r in range(rows):
        for k in range(per):
            at = here_ref[r * per + k] - step * share

            @pl.when(jnp.logical_and(at >= 0, at < share))
            def _():
                for c in range(colours):
                    total[c, at] += arr_ref[c, r, k].astype(jnp.float32)

    basis = total.shape[3]
    for t in range(share):
        factor = albedo_ref[t]
        for c in range(colours):
            lane = slice(c * basis, (c + 1) * basis)
            out_ref[t, :, lane] = (
                total[c, t] * factor[:, c : c + 1] + emission_ref[t, :, lane].astype(jnp.float32)
            ).astype(out_ref.dtype)


def per_device(blocks, row_index, col_index, send_tiles, lighting, albedo, emission):
    count, tile = blocks.shape[:2]
    width = lighting.shape[1]
    colours = albedo.shape[0]
    basis = width // colours
    listed = send_tiles.shape[0]
    rows = lax.axis_size("prow")
    n = lax.axis_size("pcol")
    tiles = lighting.shape[0] // tile
    owned = emission.shape[0] // tile
    per = listed // rows
    prow = lax.axis_index("prow")
    pcol = lax.axis_index("pcol")
    groups = (count + listed * (GROUP - 1)) // GROUP

    first = jnp.sum((row_index[None, :] < send_tiles[:, None]).astype(jnp.int32), axis=1)
    past = jnp.sum((row_index[None, :] <= send_tiles[:, None]).astype(jnp.int32), axis=1)
    needed = (past - first + GROUP - 1) // GROUP
    order = jnp.arange(listed)
    ends = jnp.sum(jnp.where(order[None, :] <= order[:, None], needed[None, :], 0), axis=1)
    starts = ends - needed
    index = jnp.arange(groups)[:, None]
    inside = jnp.logical_and(index >= starts[None, :], index < ends[None, :])
    base = jnp.sum(jnp.where(inside, first[None, :] + (index - starts[None, :]) * GROUP, 0), axis=1)
    limit = jnp.sum(jnp.where(inside, past[None, :], 0), axis=1)
    keep = jnp.sum(jnp.where(jnp.logical_and(inside, index > starts[None, :]), 1, 0), axis=1)
    plan = jnp.stack([base, limit, keep])
    local_cols = col_index - prow * (n * tiles)
    ids = jnp.broadcast_to(jnp.pad(send_tiles, (0, 128 - listed))[None, :], (8, 128))

    half = tile * basis
    slab_bytes = n * tiles * half * 2 * colours
    vmem = (count + 1) * tile * tile * 2 + slab_bytes + (groups + 1) * half * 4 + colours * listed * half * 2
    smem = pl.BlockSpec(memory_space=pltpu.SMEM)
    hbm = pl.BlockSpec(memory_space=pl.ANY)
    arrived, got = pl.pallas_call(
        functools.partial(fused, n, rows, colours),
        out_shape=(
            jax.ShapeDtypeStruct((colours, rows, per, tile, basis), jnp.bfloat16),
            jax.ShapeDtypeStruct((rows, 8, 128), jnp.int32),
        ),
        in_specs=[smem, smem, smem, hbm, hbm, hbm],
        out_specs=(hbm, hbm),
        scratch_shapes=[pltpu.VMEM((n * tiles, tile, basis), jnp.bfloat16) for _ in range(colours)]
        + [pltpu.VMEM((listed, tile, basis), jnp.bfloat16) for _ in range(colours)]
        + [
            pltpu.VMEM((count + 1, tile, tile), jnp.bfloat16),
            pltpu.VMEM((groups + 1, tile, basis), jnp.float32),
            pltpu.SemaphoreType.DMA((2, colours, n - 1)),
            pltpu.SemaphoreType.DMA((2, colours, n - 1)),
            pltpu.SemaphoreType.DMA((colours,)),
            pltpu.SemaphoreType.DMA,
            pltpu.SemaphoreType.DMA((colours, rows)),
            pltpu.SemaphoreType.DMA((colours, rows)),
            pltpu.SemaphoreType.DMA((colours,)),
            pltpu.SemaphoreType.DMA((rows,)),
            pltpu.SemaphoreType.DMA((rows,)),
            pltpu.SemaphoreType.DMA,
        ],
        compiler_params=pltpu.CompilerParams(
            collective_id=0, has_side_effects=True, vmem_limit_bytes=vmem + (2 << 20)
        ),
        cost_estimate=pl.CostEstimate(
            flops=2 * count * tile * tile * width, bytes_accessed=count * tile * tile * 2 + slab_bytes, transcendentals=0
        ),
    )(
        plan,
        ends,
        local_cols,
        ids,
        blocks,
        lighting.reshape(tiles, tile, width),
    )

    mine = lax.dynamic_slice_in_dim(got[:, 0, :], prow * per, per, axis=1)
    here = mine.reshape(-1) - (pcol * rows + prow) * owned
    share = 4
    out = pl.pallas_call(
        functools.partial(finish, share),
        out_shape=jax.ShapeDtypeStruct((owned, tile, width), jnp.bfloat16),
        grid=(owned // share,),
        in_specs=[
            smem,
            pl.BlockSpec(arrived.shape, lambda i: (0, 0, 0, 0, 0)),
            pl.BlockSpec((share, tile, colours), lambda i: (i, 0, 0)),
            pl.BlockSpec((share, tile, width), lambda i: (i, 0, 0)),
        ],
        out_specs=pl.BlockSpec((share, tile, width), lambda i: (i, 0, 0)),
        scratch_shapes=[pltpu.VMEM((colours, share, tile, basis), jnp.float32)],
        compiler_params=pltpu.CompilerParams(vmem_limit_bytes=24 << 20),
    )(
        here,
        arrived,
        jnp.transpose(albedo).reshape(owned, tile, colours),
        emission.reshape(owned, tile, width),
    )
    return out.reshape(owned * tile, width)


def solution(mesh):
    placed = (
        P(("prow", "pcol"), None, None),
        P(("prow", "pcol")),
        P(("prow", "pcol")),
        P(("prow", "pcol")),
        P(("prow", "pcol"), None),
        P(None, ("pcol", "prow")),
        P(("pcol", "prow"), None),
    )
    return jax.shard_map(
        per_device, mesh=mesh, in_specs=placed, out_specs=P(("pcol", "prow"), None), check_vma=False
    )
```

```python
import functools

import jax
import jax.numpy as jnp
from jax import lax
from jax.experimental import pallas as pl
from jax.experimental.pallas import tpu as pltpu
from jax.sharding import PartitionSpec as P

GROUP = 8
BATCH = 8
MESH = pl.DeviceIdType.MESH


def ring_place(pcol, n):
    odd = pcol % 2
    return (1 - odd) * (pcol // 2) + odd * (n - 1 - pcol // 2)


def ring_device(place, n):
    late = place // (n // 2)
    return (1 - late) * (2 * place) + late * (2 * (n - 1 - place) + 1)


def fused(
    n,
    rows,
    colours,
    plan_ref,
    last_ref,
    col_ref,
    ids_ref,
    blocks_ref,
    light_ref,
    arr_ref,
    got_ref,
    *scratch,
):
    slabs = scratch[:colours]
    parts = scratch[colours : 2 * colours]
    blk, sums, ring_send, ring_recv, own_sem, blk_sem, ex_send, ex_recv, ex_own, id_send, id_recv, id_own = scratch[
        2 * colours :
    ]
    count = blocks_ref.shape[0]
    groups = plan_ref.shape[1]
    tiles = light_ref.shape[0]
    half = tiles // 2
    listed = last_ref.shape[0]
    per = listed // rows
    basis = slabs[0].shape[2]
    prow = lax.axis_index("prow")
    pcol = lax.axis_index("pcol")
    place = ring_place(pcol, n)
    after = ring_device((place + 1) % n, n)
    before = ring_device((place + n - 1) % n, n)
    messages = n - 1

    barrier = pltpu.get_barrier_semaphore()
    for side in (after, before):
        pl.semaphore_signal(barrier, inc=1, device_id={"pcol": side}, device_id_type=MESH)
    for d in range(1, rows):
        pl.semaphore_signal(barrier, inc=1, device_id={"prow": (prow + d) % rows}, device_id_type=MESH)

    own = [
        pltpu.make_async_copy(
            light_ref.at[:, :, pl.ds(c * basis, basis)], slabs[c].at[pl.ds(pcol * tiles, tiles)], own_sem.at[c]
        )
        for c in range(colours)
    ]
    for copy in own:
        copy.start()
    pl.semaphore_wait(barrier, 2 + rows - 1)

    def piece(c, m, way, arriving):
        step = m // 2
        part = (m + way) % 2
        if way == 0:
            source = (place + n - step - arriving) % n
        else:
            source = (place + step + arriving) % n
        at = ring_device(source, n) * tiles + part * half
        window = slabs[c].at[pl.ds(at, half)]
        return pltpu.make_async_remote_copy(
            src_ref=window,
            dst_ref=window,
            send_sem=ring_send.at[way, c, m],
            recv_sem=ring_recv.at[way, c, m],
            device_id={"pcol": before if way else after},
            device_id_type=MESH,
        )

    def to_row(c, d):
        target = (prow + d) % rows
        return pltpu.make_async_remote_copy(
            src_ref=parts[c].at[pl.ds(target * per, per)],
            dst_ref=arr_ref.at[c, prow],
            send_sem=ex_send.at[c, d],
            recv_sem=ex_recv.at[c, d],
            device_id={"prow": target},
            device_id_type=MESH,
        )

    def from_row(c, d):
        origin = (prow + rows - d) % rows
        return pltpu.make_async_remote_copy(
            src_ref=parts[c].at[pl.ds(0, per)],
            dst_ref=arr_ref.at[c, origin],
            send_sem=ex_send.at[c, d],
            recv_sem=ex_recv.at[c, d],
            device_id={"prow": origin},
            device_id_type=MESH,
        )

    def ids_to(d):
        target = (prow + d) % rows
        return pltpu.make_async_remote_copy(
            src_ref=ids_ref,
            dst_ref=got_ref.at[prow],
            send_sem=id_send.at[d],
            recv_sem=id_recv.at[d],
            device_id={"prow": target},
            device_id_type=MESH,
        )

    def ids_from(d):
        origin = (prow + rows - d) % rows
        return pltpu.make_async_remote_copy(
            src_ref=ids_ref,
            dst_ref=got_ref.at[origin],
            send_sem=id_send.at[d],
            recv_sem=id_recv.at[d],
            device_id={"prow": origin},
            device_id_type=MESH,
        )

    load = pltpu.make_async_copy(blocks_ref, blk.at[pl.ds(0, count)], blk_sem)

    def compute(c, low, high):
        def one(i, running):
            products = []
            for u in range(BATCH):
                base = plan_ref[0, i * BATCH + u]
                end = plan_ref[1, i * BATCH + u]
                left, right = [], []
                for j in range(GROUP):
                    at = base + j
                    inside = at < end
                    left.append(blk[jnp.where(inside, at, count)])
                    right.append(slabs[c][col_ref[jnp.where(inside, at, 0)]])
                products.append(
                    jnp.dot(
                        jnp.concatenate(left, axis=1),
                        jnp.concatenate(right, axis=0),
                        preferred_element_type=jnp.float32,
                    )
                )
            for u in range(BATCH):
                running = running * plan_ref[2, i * BATCH + u].astype(jnp.float32) + products[u]
                sums[i * BATCH + u + 1] = running
            return running

        lax.fori_loop(low, high, one, sums[low * BATCH])

    def exchange(c):
        for s in range(listed):
            parts[c][s] = sums[last_ref[s]].astype(jnp.bfloat16)
        for d in range(1, rows):
            to_row(c, d).start()
        pltpu.make_async_copy(parts[c].at[pl.ds(prow * per, per)], arr_ref.at[c, prow], ex_own.at[c]).start()

    def finish_ring(c):
        for m in range(max(messages - 2, 0), messages):
            for way in (0, 1):
                piece(c, m, way, 1).wait_recv()

    batches = groups // BATCH
    cuts = [batches * k // (messages - 1) for k in range(messages)]
    for c in range(colours):
        own[c].wait()
        for m in range(messages):
            for way in (0, 1):
                if m >= 2:
                    piece(c, m - 2, way, 1).wait_recv()
                piece(c, m, way, 0).start()
            if c == 0 and m == 1:
                load.start()
                blk[count] = jnp.zeros(blk.shape[1:], blk.dtype)
                sums[0] = jnp.zeros(sums.shape[1:], sums.dtype)
                for d in range(1, rows):
                    ids_to(d).start()
                pltpu.make_async_copy(ids_ref, got_ref.at[prow], id_own).start()
            if c >= 1 and m >= 1:
                if m == 1:
                    if c == 1:
                        load.wait()
                    finish_ring(c - 1)
                compute(c - 1, cuts[m - 1], cuts[m])
                if m == messages - 1:
                    exchange(c - 1)
    finish_ring(colours - 1)
    compute(colours - 1, 0, batches)
    exchange(colours - 1)
    for c in range(colours):
        for m in range(messages):
            for way in (0, 1):
                piece(c, m, way, 0).wait_send()
        for d in range(1, rows):
            to_row(c, d).wait_send()
            from_row(c, d).wait_recv()
        pltpu.make_async_copy(parts[c].at[pl.ds(prow * per, per)], arr_ref.at[c, prow], ex_own.at[c]).wait()
    for d in range(1, rows):
        ids_to(d).wait_send()
        ids_from(d).wait_recv()
    pltpu.make_async_copy(ids_ref, got_ref.at[prow], id_own).wait()


def finish(share, here_ref, arr_ref, albedo_ref, emission_ref, out_ref, total):
    colours, rows, per = arr_ref.shape[:3]
    step = pl.program_id(0)
    total[...] = jnp.zeros_like(total)
    for r in range(rows):
        for k in range(per):
            at = here_ref[r * per + k] - step * share

            @pl.when(jnp.logical_and(at >= 0, at < share))
            def _():
                for c in range(colours):
                    total[c, at] += arr_ref[c, r, k].astype(jnp.float32)

    basis = total.shape[3]
    for t in range(share):
        factor = albedo_ref[t]
        for c in range(colours):
            lane = slice(c * basis, (c + 1) * basis)
            out_ref[t, :, lane] = (
                total[c, t] * factor[:, c : c + 1] + emission_ref[t, :, lane].astype(jnp.float32)
            ).astype(out_ref.dtype)


def per_device(blocks, row_index, col_index, send_tiles, lighting, albedo, emission):
    count, tile = blocks.shape[:2]
    width = lighting.shape[1]
    colours = albedo.shape[0]
    basis = width // colours
    listed = send_tiles.shape[0]
    rows = lax.axis_size("prow")
    n = lax.axis_size("pcol")
    tiles = lighting.shape[0] // tile
    owned = emission.shape[0] // tile
    per = listed // rows
    prow = lax.axis_index("prow")
    pcol = lax.axis_index("pcol")
    groups = (count + listed * (GROUP - 1)) // GROUP
    groups = -(-groups // BATCH) * BATCH

    first = jnp.sum((row_index[None, :] < send_tiles[:, None]).astype(jnp.int32), axis=1)
    past = jnp.sum((row_index[None, :] <= send_tiles[:, None]).astype(jnp.int32), axis=1)
    needed = (past - first + GROUP - 1) // GROUP
    order = jnp.arange(listed)
    ends = jnp.sum(jnp.where(order[None, :] <= order[:, None], needed[None, :], 0), axis=1)
    starts = ends - needed
    index = jnp.arange(groups)[:, None]
    inside = jnp.logical_and(index >= starts[None, :], index < ends[None, :])
    base = jnp.sum(jnp.where(inside, first[None, :] + (index - starts[None, :]) * GROUP, 0), axis=1)
    limit = jnp.sum(jnp.where(inside, past[None, :], 0), axis=1)
    keep = jnp.sum(jnp.where(jnp.logical_and(inside, index > starts[None, :]), 1, 0), axis=1)
    plan = jnp.stack([base, limit, keep])
    local_cols = col_index - prow * (n * tiles)
    ids = jnp.broadcast_to(jnp.pad(send_tiles, (0, 128 - listed))[None, :], (8, 128))

    half = tile * basis
    slab_bytes = n * tiles * half * 2 * colours
    vmem = (count + 1) * tile * tile * 2 + slab_bytes + (groups + 1) * half * 4 + colours * listed * half * 2
    smem = pl.BlockSpec(memory_space=pltpu.SMEM)
    hbm = pl.BlockSpec(memory_space=pl.ANY)
    arrived, got = pl.pallas_call(
        functools.partial(fused, n, rows, colours),
        out_shape=(
            jax.ShapeDtypeStruct((colours, rows, per, tile, basis), jnp.bfloat16),
            jax.ShapeDtypeStruct((rows, 8, 128), jnp.int32),
        ),
        in_specs=[smem, smem, smem, hbm, hbm, hbm],
        out_specs=(hbm, hbm),
        scratch_shapes=[pltpu.VMEM((n * tiles, tile, basis), jnp.bfloat16) for _ in range(colours)]
        + [pltpu.VMEM((listed, tile, basis), jnp.bfloat16) for _ in range(colours)]
        + [
            pltpu.VMEM((count + 1, tile, tile), jnp.bfloat16),
            pltpu.VMEM((groups + 1, tile, basis), jnp.float32),
            pltpu.SemaphoreType.DMA((2, colours, n - 1)),
            pltpu.SemaphoreType.DMA((2, colours, n - 1)),
            pltpu.SemaphoreType.DMA((colours,)),
            pltpu.SemaphoreType.DMA,
            pltpu.SemaphoreType.DMA((colours, rows)),
            pltpu.SemaphoreType.DMA((colours, rows)),
            pltpu.SemaphoreType.DMA((colours,)),
            pltpu.SemaphoreType.DMA((rows,)),
            pltpu.SemaphoreType.DMA((rows,)),
            pltpu.SemaphoreType.DMA,
        ],
        compiler_params=pltpu.CompilerParams(
            collective_id=0, has_side_effects=True, vmem_limit_bytes=max(vmem + (2 << 20), 58 << 20)
        ),
        cost_estimate=pl.CostEstimate(
            flops=2 * count * tile * tile * width, bytes_accessed=count * tile * tile * 2 + slab_bytes, transcendentals=0
        ),
    )(
        plan,
        ends,
        local_cols,
        ids,
        blocks,
        lighting.reshape(tiles, tile, width),
    )

    mine = lax.dynamic_slice_in_dim(got[:, 0, :], prow * per, per, axis=1)
    here = mine.reshape(-1) - (pcol * rows + prow) * owned
    share = 4
    out = pl.pallas_call(
        functools.partial(finish, share),
        out_shape=jax.ShapeDtypeStruct((owned, tile, width), jnp.bfloat16),
        grid=(owned // share,),
        in_specs=[
            smem,
            pl.BlockSpec(arrived.shape, lambda i: (0, 0, 0, 0, 0)),
            pl.BlockSpec((share, tile, colours), lambda i: (i, 0, 0)),
            pl.BlockSpec((share, tile, width), lambda i: (i, 0, 0)),
        ],
        out_specs=pl.BlockSpec((share, tile, width), lambda i: (i, 0, 0)),
        scratch_shapes=[pltpu.VMEM((colours, share, tile, basis), jnp.float32)],
        compiler_params=pltpu.CompilerParams(vmem_limit_bytes=24 << 20),
    )(
        here,
        arrived,
        jnp.transpose(albedo).reshape(owned, tile, colours),
        emission.reshape(owned, tile, width),
    )
    return out.reshape(owned * tile, width)


def solution(mesh):
    placed = (
        P(("prow", "pcol"), None, None),
        P(("prow", "pcol")),
        P(("prow", "pcol")),
        P(("prow", "pcol")),
        P(("prow", "pcol"), None),
        P(None, ("pcol", "prow")),
        P(("pcol", "prow"), None),
    )
    return jax.shard_map(
        per_device, mesh=mesh, in_specs=placed, out_specs=P(("pcol", "prow"), None), check_vma=False
    )
```

```python
import functools

import jax
import jax.numpy as jnp
from jax import lax
from jax.experimental import pallas as pl
from jax.experimental.pallas import tpu as pltpu
from jax.sharding import PartitionSpec as P

GROUP = 8
BATCH = 8
MESH = pl.DeviceIdType.MESH


def ring_place(pcol, n):
    odd = pcol % 2
    return (1 - odd) * (pcol // 2) + odd * (n - 1 - pcol // 2)


def ring_device(place, n):
    late = place // (n // 2)
    return (1 - late) * (2 * place) + late * (2 * (n - 1 - place) + 1)


def fused(
    n,
    rows,
    colours,
    plan_ref,
    last_ref,
    col_ref,
    ids_ref,
    blocks_ref,
    light_ref,
    arr_ref,
    got_ref,
    *scratch,
):
    slabs = scratch[:colours]
    parts = scratch[colours : 2 * colours]
    blk, sums, ring_send, ring_recv, own_sem, blk_sem, ex_send, ex_recv, ex_own, id_send, id_recv, id_own = scratch[
        2 * colours :
    ]
    count = blocks_ref.shape[0]
    groups = plan_ref.shape[1]
    tiles = light_ref.shape[0]
    half = tiles // 2
    listed = last_ref.shape[0]
    per = listed // rows
    basis = slabs[0].shape[2]
    prow = lax.axis_index("prow")
    pcol = lax.axis_index("pcol")
    place = ring_place(pcol, n)
    after = ring_device((place + 1) % n, n)
    before = ring_device((place + n - 1) % n, n)
    messages = n - 1

    barrier = pltpu.get_barrier_semaphore()
    for side in (after, before):
        pl.semaphore_signal(barrier, inc=1, device_id={"pcol": side}, device_id_type=MESH)
    for d in range(1, rows):
        pl.semaphore_signal(barrier, inc=1, device_id={"prow": (prow + d) % rows}, device_id_type=MESH)

    own = [
        pltpu.make_async_copy(
            light_ref.at[:, :, pl.ds(c * basis, basis)], slabs[c].at[pl.ds(pcol * tiles, tiles)], own_sem.at[c]
        )
        for c in range(colours)
    ]
    for copy in own:
        copy.start()
    pl.semaphore_wait(barrier, 2 + rows - 1)

    def piece(c, m, way, arriving):
        step = m // 2
        part = (m + way) % 2
        if way == 0:
            source = (place + n - step - arriving) % n
        else:
            source = (place + step + arriving) % n
        at = ring_device(source, n) * tiles + part * half
        window = slabs[c].at[pl.ds(at, half)]
        return pltpu.make_async_remote_copy(
            src_ref=window,
            dst_ref=window,
            send_sem=ring_send.at[way, c, m],
            recv_sem=ring_recv.at[way, c, m],
            device_id={"pcol": before if way else after},
            device_id_type=MESH,
        )

    def to_row(c, d):
        target = (prow + d) % rows
        return pltpu.make_async_remote_copy(
            src_ref=parts[c].at[pl.ds(target * per, per)],
            dst_ref=arr_ref.at[c, prow],
            send_sem=ex_send.at[c, d],
            recv_sem=ex_recv.at[c, d],
            device_id={"prow": target},
            device_id_type=MESH,
        )

    def from_row(c, d):
        origin = (prow + rows - d) % rows
        return pltpu.make_async_remote_copy(
            src_ref=parts[c].at[pl.ds(0, per)],
            dst_ref=arr_ref.at[c, origin],
            send_sem=ex_send.at[c, d],
            recv_sem=ex_recv.at[c, d],
            device_id={"prow": origin},
            device_id_type=MESH,
        )

    def ids_to(d):
        target = (prow + d) % rows
        return pltpu.make_async_remote_copy(
            src_ref=ids_ref,
            dst_ref=got_ref.at[prow],
            send_sem=id_send.at[d],
            recv_sem=id_recv.at[d],
            device_id={"prow": target},
            device_id_type=MESH,
        )

    def ids_from(d):
        origin = (prow + rows - d) % rows
        return pltpu.make_async_remote_copy(
            src_ref=ids_ref,
            dst_ref=got_ref.at[origin],
            send_sem=id_send.at[d],
            recv_sem=id_recv.at[d],
            device_id={"prow": origin},
            device_id_type=MESH,
        )

    load = pltpu.make_async_copy(blocks_ref, blk.at[pl.ds(0, count)], blk_sem)

    def compute(c, low, high):
        def one(i, running):
            products = []
            for u in range(BATCH):
                base = plan_ref[0, i * BATCH + u]
                end = plan_ref[1, i * BATCH + u]
                left, right = [], []
                for j in range(GROUP):
                    at = base + j
                    inside = at < end
                    left.append(blk[jnp.where(inside, at, count)])
                    right.append(slabs[c][col_ref[jnp.where(inside, at, 0)]])
                products.append(
                    jnp.dot(
                        jnp.concatenate(left, axis=1),
                        jnp.concatenate(right, axis=0),
                        preferred_element_type=jnp.float32,
                    )
                )
            for u in range(BATCH):
                running = running * plan_ref[2, i * BATCH + u].astype(jnp.float32) + products[u]
                sums[i * BATCH + u + 1] = running
            return running

        lax.fori_loop(low, high, one, sums[low * BATCH])

    def exchange(c):
        for s in range(listed):
            parts[c][s] = sums[last_ref[s]].astype(jnp.bfloat16)
        for d in range(1, rows):
            to_row(c, d).start()
        pltpu.make_async_copy(parts[c].at[pl.ds(prow * per, per)], arr_ref.at[c, prow], ex_own.at[c]).start()

    def finish_ring(c):
        for m in range(max(messages - 2, 0), messages):
            for way in (0, 1):
                piece(c, m, way, 1).wait_recv()

    batches = groups // BATCH
    cuts = [batches * k // (messages - 1) for k in range(messages)]
    for c in range(colours):
        own[c].wait()
        for m in range(messages):
            for way in (0, 1):
                if m >= 2:
                    piece(c, m - 2, way, 1).wait_recv()
                piece(c, m, way, 0).start()
            if c == 0 and m == 1:
                load.start()
                blk[count] = jnp.zeros(blk.shape[1:], blk.dtype)
                sums[0] = jnp.zeros(sums.shape[1:], sums.dtype)
                for d in range(1, rows):
                    ids_to(d).start()
                pltpu.make_async_copy(ids_ref, got_ref.at[prow], id_own).start()
            if c >= 1 and m >= 1:
                if m == 1:
                    if c == 1:
                        load.wait()
                    finish_ring(c - 1)
                compute(c - 1, cuts[m - 1], cuts[m])
                if m == messages - 1:
                    exchange(c - 1)
    finish_ring(colours - 1)
    compute(colours - 1, 0, batches)
    exchange(colours - 1)
    for c in range(colours):
        for m in range(messages):
            for way in (0, 1):
                piece(c, m, way, 0).wait_send()
        for d in range(1, rows):
            to_row(c, d).wait_send()
            from_row(c, d).wait_recv()
        pltpu.make_async_copy(parts[c].at[pl.ds(prow * per, per)], arr_ref.at[c, prow], ex_own.at[c]).wait()
    for d in range(1, rows):
        ids_to(d).wait_send()
        ids_from(d).wait_recv()
    pltpu.make_async_copy(ids_ref, got_ref.at[prow], id_own).wait()


def finish(here_ref, arr_ref, albedo_ref, emission_ref, out_ref, total):
    rows, per = arr_ref.shape[1:3]
    step = pl.program_id(0)
    total[...] = jnp.zeros_like(total)
    for r in range(rows):
        for k in range(per):
            total[here_ref[r * per + k]] += arr_ref[0, r, k].astype(jnp.float32)
    for c in range(albedo_ref.shape[2]):

        @pl.when(step == c)
        def _():
            for t in range(total.shape[0]):
                lit = total[t] * albedo_ref[t][:, c : c + 1] + emission_ref[t].astype(jnp.float32)
                out_ref[t] = lit.astype(out_ref.dtype)


def per_device(blocks, row_index, col_index, send_tiles, lighting, albedo, emission):
    count, tile = blocks.shape[:2]
    width = lighting.shape[1]
    colours = albedo.shape[0]
    basis = width // colours
    listed = send_tiles.shape[0]
    rows = lax.axis_size("prow")
    n = lax.axis_size("pcol")
    tiles = lighting.shape[0] // tile
    owned = emission.shape[0] // tile
    per = listed // rows
    prow = lax.axis_index("prow")
    pcol = lax.axis_index("pcol")
    groups = (count + listed * (GROUP - 1)) // GROUP
    groups = -(-groups // BATCH) * BATCH

    first = jnp.sum((row_index[None, :] < send_tiles[:, None]).astype(jnp.int32), axis=1)
    past = jnp.sum((row_index[None, :] <= send_tiles[:, None]).astype(jnp.int32), axis=1)
    needed = (past - first + GROUP - 1) // GROUP
    order = jnp.arange(listed)
    ends = jnp.sum(jnp.where(order[None, :] <= order[:, None], needed[None, :], 0), axis=1)
    starts = ends - needed
    index = jnp.arange(groups)[:, None]
    inside = jnp.logical_and(index >= starts[None, :], index < ends[None, :])
    base = jnp.sum(jnp.where(inside, first[None, :] + (index - starts[None, :]) * GROUP, 0), axis=1)
    limit = jnp.sum(jnp.where(inside, past[None, :], 0), axis=1)
    keep = jnp.sum(jnp.where(jnp.logical_and(inside, index > starts[None, :]), 1, 0), axis=1)
    plan = jnp.stack([base, limit, keep])
    local_cols = col_index - prow * (n * tiles)
    ids = jnp.broadcast_to(jnp.pad(send_tiles, (0, 128 - listed))[None, :], (8, 128))

    half = tile * basis
    slab_bytes = n * tiles * half * 2 * colours
    vmem = (count + 1) * tile * tile * 2 + slab_bytes + (groups + 1) * half * 4 + colours * listed * half * 2
    smem = pl.BlockSpec(memory_space=pltpu.SMEM)
    hbm = pl.BlockSpec(memory_space=pl.ANY)
    arrived, got = pl.pallas_call(
        functools.partial(fused, n, rows, colours),
        out_shape=(
            jax.ShapeDtypeStruct((colours, rows, per, tile, basis), jnp.bfloat16),
            jax.ShapeDtypeStruct((rows, 8, 128), jnp.int32),
        ),
        in_specs=[smem, smem, smem, hbm, hbm, hbm],
        out_specs=(hbm, hbm),
        scratch_shapes=[pltpu.VMEM((n * tiles, tile, basis), jnp.bfloat16) for _ in range(colours)]
        + [pltpu.VMEM((listed, tile, basis), jnp.bfloat16) for _ in range(colours)]
        + [
            pltpu.VMEM((count + 1, tile, tile), jnp.bfloat16),
            pltpu.VMEM((groups + 1, tile, basis), jnp.float32),
            pltpu.SemaphoreType.DMA((2, colours, n - 1)),
            pltpu.SemaphoreType.DMA((2, colours, n - 1)),
            pltpu.SemaphoreType.DMA((colours,)),
            pltpu.SemaphoreType.DMA,
            pltpu.SemaphoreType.DMA((colours, rows)),
            pltpu.SemaphoreType.DMA((colours, rows)),
            pltpu.SemaphoreType.DMA((colours,)),
            pltpu.SemaphoreType.DMA((rows,)),
            pltpu.SemaphoreType.DMA((rows,)),
            pltpu.SemaphoreType.DMA,
        ],
        compiler_params=pltpu.CompilerParams(
            collective_id=0, has_side_effects=True, vmem_limit_bytes=max(vmem + (2 << 20), 58 << 20)
        ),
        cost_estimate=pl.CostEstimate(
            flops=2 * count * tile * tile * width, bytes_accessed=count * tile * tile * 2 + slab_bytes, transcendentals=0
        ),
    )(
        plan,
        ends,
        local_cols,
        ids,
        blocks,
        lighting.reshape(tiles, tile, width),
    )

    mine = lax.dynamic_slice_in_dim(got[:, 0, :], prow * per, per, axis=1)
    here = mine.reshape(-1) - (pcol * rows + prow) * owned
    out = pl.pallas_call(
        finish,
        out_shape=jax.ShapeDtypeStruct((owned, tile, width), jnp.bfloat16),
        grid=(colours,),
        in_specs=[
            smem,
            pl.BlockSpec((1, rows, per, tile, basis), lambda i: (i, 0, 0, 0, 0)),
            pl.BlockSpec((owned, tile, colours), lambda i: (0, 0, 0)),
            pl.BlockSpec((owned, tile, basis), lambda i: (0, 0, i)),
        ],
        out_specs=pl.BlockSpec((owned, tile, basis), lambda i: (0, 0, i)),
        scratch_shapes=[pltpu.VMEM((owned, tile, basis), jnp.float32)],
        compiler_params=pltpu.CompilerParams(vmem_limit_bytes=24 << 20),
    )(
        here,
        arrived,
        jnp.transpose(albedo).reshape(owned, tile, colours),
        emission.reshape(owned, tile, width),
    )
    return out.reshape(owned * tile, width)


def solution(mesh):
    placed = (
        P(("prow", "pcol"), None, None),
        P(("prow", "pcol")),
        P(("prow", "pcol")),
        P(("prow", "pcol")),
        P(("prow", "pcol"), None),
        P(None, ("pcol", "prow")),
        P(("pcol", "prow"), None),
    )
    return jax.shard_map(
        per_device, mesh=mesh, in_specs=placed, out_specs=P(("pcol", "prow"), None), check_vma=False
    )
```
